256 devices in a mesh: kf: 64 (over z, y, core), head: 4 (over x).
Axes of the slice: x: 4, y: 4, z: 8, core: 2. Of those that a mesh axis runs over, the one named last changes fastest.
Arguments:
- key_states: bfloat16 [128, 510, 1280], P('kf', None, 'head'), may hold values from -6 to 6
- w_query: bfloat16 [1280, 1280], P(None, 'head')
- w_key: bfloat16 [1280, 1280], P(None, 'head')
- w_value: bfloat16 [1280, 1280], P(None, 'head'), may hold values from -0.15625 to 0.15625
- w_out: bfloat16 [1280, 1280], P('head'), may hold values from -0.625 to 0.625
- gain: float32 [1280], replicated, may hold values from 0.1 to 1.9
- bias: float32 [1280], replicated, may hold values from -3 to 3
- src_key: int32 [896, 510, 2], P('kf'), may hold values from 0 to 127, as said below
- src_tok: int32 [896, 510, 2], P('kf'), may hold values from 0 to 509
- weight_num: int32 [896, 510], P('kf'), may hold values from 0 to 16
Outputs:
- key_out: bfloat16 [128, 510, 1280], P('kf', None, 'head')
- blended: bfloat16 [896, 510, 1280], P('kf', None, 'head')
The draws below stay inside these ranges and needn't reach their ends.
Inputs may be any that keep to these rules, and one draw needn't show every extreme that they name: `src_key`: keyframe k lies at kf index k // 2, non-key frame f at kf index f // 14. The two source keyframes of every token of frame f are the keyframes bracketing it, f // 7 and min(f // 7 + 1, 127), in either order.
All inputs are finite; a program needn't handle non-finite values.
Results may differ from the reference program's by a relative error of at most 0.015.
Values may be sent and summed in bfloat16 or wider, within the bound.
A program may use at most 128 MiB of HBM per device.

```python
import jax
import jax.numpy as jnp
from jax import lax

D = 1280
HEADS = 20
P_SIZE = 510
BATCH = 8
NK_PER = 7
DEN = 16
HD = 64
KEYS = 128
NONKEY = 896
N_HEAD = 4


def order_flags(key):
    return jax.random.randint(jax.random.fold_in(key, 77), (NONKEY, P_SIZE), 0, 2)


def draw_w_query(key, part):
    key = jax.random.fold_in(key, 21)
    own = jax.random.normal(key, (D, D), jnp.float32)
    mixed = own * (D // 2) ** (-0.5)
    return mixed.astype(jnp.bfloat16)


def draw_w_key(key, part):
    key = jax.random.fold_in(key, 22)
    own = jax.random.normal(key, (D, D), jnp.float32)
    mixed = own * (D // 2) ** (-0.5)
    return mixed.astype(jnp.bfloat16)


def draw_src_key(key, part):
    flags = order_flags(key)
    before = jnp.arange(NONKEY, dtype=jnp.int32) // NK_PER
    after = jnp.minimum(before + 1, KEYS - 1)
    before = jnp.broadcast_to(before[:, None], (NONKEY, P_SIZE))
    after = jnp.broadcast_to(after[:, None], (NONKEY, P_SIZE))
    first = jnp.where(flags == 1, after, before)
    second = jnp.where(flags == 1, before, after)
    return jnp.stack([first, second], axis=-1).astype(jnp.int32)


def draw_weight_num(key, part):
    flags = order_flags(key)
    key = jax.random.fold_in(key, 6)
    place = jnp.arange(NONKEY, dtype=jnp.int32) % NK_PER
    base = DEN * (NK_PER - place) // (NK_PER + 1)
    base = jnp.broadcast_to(base[:, None], (NONKEY, P_SIZE))
    base = jnp.where(flags == 1, DEN - base, base)
    jitter = jax.random.randint(key, (NONKEY, P_SIZE), -2, 3)
    return jnp.clip(base + jitter, 0, DEN).astype(jnp.int32)


def set_ends(values, stream_key, least, largest):
    spot = [jax.random.randint(jax.random.fold_in(stream_key, axis), (), 0, length) for axis, length in enumerate(values.shape)]
    widest = values.shape.index(max(values.shape))
    next_to = spot[:widest] + [(spot[widest] + 1) % values.shape[widest]] + spot[widest + 1:]
    return values.at[tuple(spot)].set(least).at[tuple(next_to)].set(largest)


def steps_of(key, extent, cuts, low, largest):
    loudness = 1.0
    for dim, blocks in cuts:
        steps = jax.random.uniform(jax.random.fold_in(jax.random.fold_in(key, 6), dim), (blocks,), jnp.float32, low / len(cuts), largest / len(cuts))
        loudness = loudness * jnp.repeat(jnp.exp(steps), extent[dim] // blocks).reshape((-1,) + (1,) * (len(extent) - 1 - dim))
    return loudness


def gaussian(key, dims, scale, most, shards=(), held_as=jnp.bfloat16):
    loudness = steps_of(key, dims, shards, -0.22, 0.18) if shards else 1.0
    values = jax.random.normal(key, dims, jnp.float32) * scale * loudness
    return jnp.minimum(jnp.maximum(values, -most), most).astype(held_as)


def setup_inputs(seed: int = 0) -> dict:
    splits = jax.random.split(jax.random.key(seed), 11)
    key_states = gaussian(splits[0], (KEYS, P_SIZE, D), 1.0, 6.0, ((0, 64), (2, 4)))
    w_query = draw_w_query(jax.random.fold_in(splits[10], 71), 0)
    w_key = draw_w_key(jax.random.fold_in(splits[10], 71), 0)
    w_value = gaussian(splits[3], (D, D), D ** -0.5, 0.15625, ((1, 4),))
    w_out = gaussian(splits[4], (D, D), (D // 16) ** -0.5, 0.625, ((0, 4),))
    gain = jnp.clip(1.0 + 0.18 * jax.random.normal(splits[5], (D,), jnp.float32), 0.1, 1.9)
    bias = gaussian(splits[6], (D,), 0.5, 3.0, (), jnp.float32)
    src_key = draw_src_key(jax.random.fold_in(splits[10], 71), 0)
    src_tok = set_ends(jax.random.randint(splits[8], (NONKEY, P_SIZE, 2), 0, P_SIZE), jax.random.fold_in(splits[8], 1), 0, P_SIZE - 1).astype(jnp.int32)
    weight_num = draw_weight_num(jax.random.fold_in(splits[10], 71), 0)
    return {"key_states": key_states, "w_query": w_query, "w_key": w_key, "w_value": w_value, "w_out": w_out, "gain": gain, "bias": bias, "src_key": src_key, "src_tok": src_tok, "weight_num": weight_num}


def normalize(states, gain, bias):
    values = states.astype(jnp.float32)
    center = lax.optimization_barrier(jnp.mean(values, axis=-1, keepdims=True))
    spread = lax.optimization_barrier(jnp.mean((values - center) ** 2, axis=-1, keepdims=True))
    return ((values - center) * lax.rsqrt(spread + 1e-05) * gain + bias).astype(jnp.bfloat16)

def one_head(parts):
    query_h, key_h, value_h = parts
    scores = jnp.dot(query_h, key_h.T, preferred_element_type=jnp.float32) * HD ** (-0.5)
    top = lax.optimization_barrier(jnp.max(scores, axis=-1, keepdims=True))
    expo = jnp.exp(scores - top)
    probs = (expo / lax.optimization_barrier(jnp.sum(expo, axis=-1, keepdims=True))).astype(jnp.bfloat16)
    return jnp.dot(probs, value_h, preferred_element_type=jnp.float32).astype(jnp.bfloat16)

def batch_attention(normed, w_query, w_key, w_value, w_out):
    rows = normed.shape[0]
    query = jnp.dot(normed, w_query, preferred_element_type=jnp.float32).astype(jnp.bfloat16)
    keys = jnp.dot(normed, w_key, preferred_element_type=jnp.float32).astype(jnp.bfloat16)
    values = jnp.dot(normed, w_value, preferred_element_type=jnp.float32).astype(jnp.bfloat16)

    def split(array):
        return array.reshape(rows, HEADS, HD).transpose(1, 0, 2)
    attended = lax.map(one_head, (split(query), split(keys), split(values)))
    attended = attended.transpose(1, 0, 2).reshape(rows, D)
    grouped = attended.reshape(rows, N_HEAD, D // N_HEAD).astype(jnp.float32)
    w_grouped = w_out.reshape(N_HEAD, D // N_HEAD, D).astype(jnp.float32)
    partial_g = jnp.einsum('rgc,gce->gre', grouped, w_grouped).astype(jnp.bfloat16)
    return lax.optimization_barrier(jnp.sum(partial_g.astype(jnp.float32), axis=0)).astype(jnp.bfloat16)

def reference(key_states, w_query, w_key, w_value, w_out, gain, bias, src_key, src_tok, weight_num):
    normed = normalize(key_states, gain, bias)
    batches = normed.reshape(KEYS // BATCH, BATCH * P_SIZE, D)
    outputs = lax.map(lambda batch_rows: batch_attention(batch_rows, w_query, w_key, w_value, w_out), batches)
    key_out = outputs.reshape(KEYS, P_SIZE, D)
    flat = key_out.reshape(KEYS * P_SIZE, D)

    def frame(parts):
        keys_f, toks_f, num_f = parts
        first = flat[(keys_f[:, 0] * P_SIZE + toks_f[:, 0]).astype(jnp.int32)].astype(jnp.float32)
        second = flat[(keys_f[:, 1] * P_SIZE + toks_f[:, 1]).astype(jnp.int32)].astype(jnp.float32)
        share = num_f.astype(jnp.float32) / DEN
        return (share[:, None] * first + (1.0 - share)[:, None] * second).astype(jnp.bfloat16)
    blended = lax.map(frame, (src_key, src_tok, weight_num))
    return (key_out, blended)
```

```python
import functools

import jax
import jax.numpy as jnp
from jax import lax
from jax.experimental import pallas as pl
from jax.experimental.pallas import tpu as pltpu
from jax.sharding import PartitionSpec as P

MESH = pl.DeviceIdType.MESH
HD = 64
DEN = 16
TOK = 510
PAD = 512
QW = 2 * PAD
SCORE_SCALE = 0.125 * 1.4426950408889634
LOWEST = -3e38


def attend(n_x, x_ref, wq_hbm, wk_hbm, wv_hbm, wo_hbm, gain_ref, bias_ref, out_ref,
           wq, wk, wv, wo, xg, nt, qz, kb, vb, ones, acc, top, at, wt, wog, gb,
           w_sem, x_send, x_recv, kv_send, kv_recv, a_send, a_recv, o_send, o_recv):
    kf = lax.axis_index("kf")
    x = lax.axis_index("head")
    right, left, far = lax.rem(x + 1, n_x), lax.rem(x + 3, n_x), lax.rem(x + 2, n_x)
    core = kf + 1 - 2 * lax.rem(kf, 2)
    ymate = kf + 2 - 4 * lax.rem(kf // 2, 2)
    dev_r, dev_l, dev_far, dev_core, dev_y = (kf, right), (kf, left), (kf, far), (core, x), (ymate, x)
    width = x_ref.shape[1]

    def copy(src, dst, send, recv, dev):
        return pltpu.make_async_remote_copy(
            src_ref=src, dst_ref=dst, send_sem=send, recv_sem=recv, device_id=dev, device_id_type=MESH)

    barrier = pltpu.get_barrier_semaphore()
    for dev in (dev_r, dev_l, dev_far, dev_core, dev_y):
        pl.semaphore_signal(barrier, inc=1, device_id=dev, device_id_type=MESH)

    loads = [pltpu.make_async_copy(a, b, w_sem.at[i])
             for i, (a, b) in enumerate(((wq_hbm, wq), (wk_hbm, wk), (wv_hbm, wv), (wo_hbm, wo)))]
    for load in loads:
        load.start()

    def xrow(owner, half=None):
        if half is None:
            return pl.ds(pl.multiple_of(owner * width, 64), width)
        return pl.ds(pl.multiple_of(owner * width + half * (width // 2), 32), width // 2)

    for f in range(2):
        xg[f, xrow(x), pl.ds(PAD - 128, 128)] = jnp.zeros((width, 128), jnp.bfloat16)
        xg[f, xrow(x), pl.ds(0, TOK)] = x_ref[f]
    pl.semaphore_wait(barrier, 5)

    def x_own(f):
        piece = xg.at[f, xrow(x)]
        return (copy(piece, piece, x_send.at[f, 0], x_recv.at[f, 0], dev_r),
                copy(piece, piece, x_send.at[f, 1], x_recv.at[f, 1], dev_l))

    def x_fwd(f):
        a, b = xg.at[f, xrow(left, 0)], xg.at[f, xrow(right, 1)]
        return (copy(a, a, x_send.at[f, 2], x_recv.at[f, 2], dev_r),
                copy(b, b, x_send.at[f, 3], x_recv.at[f, 3], dev_l))

    def x_arrive(f):
        a, b = xg.at[f, xrow(left)], xg.at[f, xrow(right)]
        copy(a, a, x_send.at[f, 0], x_recv.at[f, 0], dev_l).wait_recv()
        x_fwd(f)[0].start()
        copy(b, b, x_send.at[f, 1], x_recv.at[f, 1], dev_r).wait_recv()
        x_fwd(f)[1].start()

    def x_last(f):
        a, b = xg.at[f, xrow(far, 0)], xg.at[f, xrow(far, 1)]
        copy(a, a, x_send.at[f, 2], x_recv.at[f, 2], dev_l).wait_recv()
        copy(b, b, x_send.at[f, 3], x_recv.at[f, 3], dev_r).wait_recv()

    for c in x_own(0):
        c.start()

    gb[...] = jnp.concatenate([jnp.broadcast_to(gain_ref[...], (8, gain_ref.shape[1])).T[:, 0:1],
                               jnp.broadcast_to(bias_ref[...], (8, bias_ref.shape[1])).T[:, 0:1]], axis=1)
    qz[...] = jnp.zeros_like(qz)
    row = lax.broadcasted_iota(jnp.int32, (16, QW), 0)
    col = lax.broadcasted_iota(jnp.int32, (16, QW), 1)
    ones[0] = jnp.where((row == 0) & (col % PAD < TOK), 1.0, 0.0).astype(jnp.bfloat16)
    ones[1] = jnp.where((row == 0) & ((col < PAD) | (col % 256 < 254)), 1.0, 0.0).astype(jnp.bfloat16)
    loads[3].wait()
    for j in range(n_x):
        part = wo[:, j * width:(j + 1) * width].astype(jnp.float32)
        wt[j] = part.T.astype(jnp.bfloat16)
    wog[x] = wt[x]

    x_arrive(0)
    for c in x_own(1):
        c.start()
    for load in loads[:3]:
        load.wait()

    def project(f):
        def norm(i, _):
            cols = pl.ds(pl.multiple_of(i * 128, 128), 128)
            values = xg[f, :, cols].astype(jnp.float32)
            center = jnp.mean(values, axis=0, keepdims=True)
            off = values - center
            spread = jnp.mean(off * off, axis=0, keepdims=True)
            nt[:, cols] = (off * lax.rsqrt(spread + 1e-05) * gb[:, 0:1] + gb[:, 1:2]).astype(jnp.bfloat16)
            return 0

        lax.fori_loop(0, PAD // 128, norm, 0)
        here = pl.ds(f * PAD, PAD)
        lane = lax.broadcasted_iota(jnp.int32, (width, PAD), 1)
        k = jnp.dot(wk[...], nt[...], preferred_element_type=jnp.float32)
        k = jnp.where(lane < TOK, k, k[:, TOK - 1:TOK]).T.astype(jnp.bfloat16)
        kb[0, f, 0:512, :] = k[:, 0:128]
        kb[0, f, 512:1024, :] = k[:, 128:256]
        kb[0, f, 1024:1280, :] = jnp.concatenate([k[0:256, 256:320], k[256:512, 256:320]], axis=1)
        v = jnp.dot(wv[...], nt[...], preferred_element_type=jnp.float32)
        vb[0, f] = jnp.where(lane < TOK, v, 0.0).astype(jnp.bfloat16)
        for part in pieces(f):
            for c in kv_copies(f, part, 0):
                c.start()
            for c in kv_copies(f, part, 1):
                c.start()
        q = (jnp.dot(wq[...], nt[...], preferred_element_type=jnp.float32) * SCORE_SCALE).astype(jnp.bfloat16)
        for h in range(5):
            half = (h % 2) * HD
            qz[h, half:half + HD, here] = q[h * HD:(h + 1) * HD]
        qz[5, HD:2 * HD, here] = q[4 * HD:5 * HD]

    def pieces(f):
        return (3,) if f == 0 else (0, 1, 2)

    def kv_rows(part):
        if isinstance(part, int):
            return ((pl.ds(0, 1280), pl.ds(0, 320)) if part == 3 else
                    (pl.ds(1024, 256), pl.ds(256, 64)) if part == 2 else
                    (pl.ds(part * 512, 512), pl.ds(part * 128, 128)))
        return pl.ds(pl.multiple_of(part * 512, 512), 512), pl.ds(pl.multiple_of(part * 128, 128), 128)

    def kv_copies(f, part, route, landed=False):
        k_rows, v_rows = kv_rows(part)
        source, target = (0, 0, 2)[route], (1, 2, 3)[route]
        source = target if landed else source
        dev = dev_y if route == 1 else dev_core
        return (copy(kb.at[source, f, k_rows], kb.at[target, f, k_rows],
                     kv_send.at[route, part, 0], kv_recv.at[route, part, 0], dev),
                copy(vb.at[source, f, v_rows], vb.at[target, f, v_rows],
                     kv_send.at[route, part, 1], kv_recv.at[route, part, 1], dev))

    def kv_wait(f, part, route):
        for c in kv_copies(f, part, route, landed=True):
            c.wait_recv()

    def kv_forward(f, part):
        kv_wait(f, part, 1)
        for c in kv_copies(f, part, 2):
            c.start()

    def update(h, s, values, first):
        m0 = jnp.full((1, QW), LOWEST, jnp.float32) if first else top[h]
        m = jnp.maximum(m0, jnp.max(s, axis=0, keepdims=True))
        p = jnp.exp2(s - m).astype(jnp.bfloat16)
        term = jnp.dot(values, p, preferred_element_type=jnp.float32)
        acc[h] = term if first else acc[h] * jnp.exp2(m0 - m) + term
        top[h] = m

    def block(src, h, first=False):
        rows = pl.ds(pl.multiple_of(h // 2 * 512, 512), 512)
        chans = pl.ds(pl.multiple_of(h * HD, HD), HD)
        keys = jnp.concatenate([kb[src, 0, rows, :], kb[src, 1, rows, :]], axis=0)
        vals = jnp.concatenate([vb[src, 0, chans, :], vb[src, 1, chans, :]], axis=1)
        s = jnp.dot(keys, qz[h], preferred_element_type=jnp.float32)
        update(h, s, jnp.concatenate([vals, ones[0]], axis=0), first)

    def block_last(src, first=False):
        keys = jnp.concatenate([kb[src, 0, 1024:1280, :], kb[src, 1, 1024:1280, :]], axis=0)
        vals = jnp.concatenate([vb[src, 0, 256:320, 0:256], vb[src, 1, 256:320, 0:256],
                                vb[src, 0, 256:320, 256:512], vb[src, 1, 256:320, 256:512]], axis=1)
        s = jnp.concatenate([jnp.dot(keys, qz[4], preferred_element_type=jnp.float32),
                             jnp.dot(keys, qz[5], preferred_element_type=jnp.float32)], axis=0)
        update(4, s, jnp.concatenate([vals, ones[1]], axis=0), first)

    def a_row(h, half=None):
        if half is None:
            return pl.ds(pl.multiple_of(h * HD, HD), HD)
        return pl.ds(pl.multiple_of(h * HD + half * 32, 32), 32)

    def a_own(h):
        piece = at.at[x, a_row(h)]
        return (copy(piece, piece, a_send.at[h, 0], a_recv.at[h, 0], dev_r),
                copy(piece, piece, a_send.at[h, 1], a_recv.at[h, 1], dev_l))

    def a_fwd(h):
        a, b = at.at[left, a_row(h, 0)], at.at[right, a_row(h, 1)]
        return (copy(a, a, a_send.at[h, 2], a_recv.at[h, 2], dev_r),
                copy(b, b, a_send.at[h, 3], a_recv.at[h, 3], dev_l))

    def a_arrive(h):
        a, b = at.at[left, a_row(h)], at.at[right, a_row(h)]
        copy(a, a, a_send.at[h, 0], a_recv.at[h, 0], dev_l).wait_recv()
        a_fwd(h)[0].start()
        copy(b, b, a_send.at[h, 1], a_recv.at[h, 1], dev_r).wait_recv()
        a_fwd(h)[1].start()

    def a_last(h):
        a, b = at.at[far, a_row(h, 0)], at.at[far, a_row(h, 1)]
        copy(a, a, a_send.at[h, 2], a_recv.at[h, 2], dev_l).wait_recv()
        copy(b, b, a_send.at[h, 3], a_recv.at[h, 3], dev_r).wait_recv()

    def finish(h):
        at[x, a_row(h), :] = (acc[h, 0:HD, :] / acc[h, HD:HD + 1, :]).astype(jnp.bfloat16)
        for c in a_own(h):
            c.start()

    x_last(0)
    project(0)
    x_arrive(1)
    x_last(1)
    project(1)

    def o_copies():
        return [copy(wt.at[to], wog.at[x], o_send.at[i], o_recv.at[i], (kf, to))
                for i, to in enumerate((right, far, left))]

    for c in o_copies():
        c.start()

    def own(h, _):
        block(0, h, True)
        return 0

    lax.fori_loop(0, 4, own, 0)
    block_last(0, True)

    kv_forward(0, 3)
    kv_wait(0, 3, 0)

    def pair(p, _):
        kv_forward(1, p)
        kv_wait(1, p, 0)

        def core_block(i, _):
            block(1, 2 * p + i)
            return 0

        lax.fori_loop(0, 2, core_block, 0)

        @pl.when(p == 0)
        def _():
            kv_wait(0, 3, 2)

        kv_wait(1, p, 2)

        def head(i, _):
            h = 2 * p + i

            def far_block(src, _):
                block(src, h)
                return 0

            lax.fori_loop(2, 4, far_block, 0)
            finish(h)

            @pl.when(h > 0)
            def _():
                a_arrive(h - 1)
            return 0

        lax.fori_loop(0, 2, head, 0)
        return 0

    lax.fori_loop(0, 2, pair, 0)
    kv_forward(1, 2)
    kv_wait(1, 2, 0)
    block_last(1)
    kv_wait(1, 2, 2)
    block_last(2)
    a_arrive(3)
    block_last(3)
    finish(4)

    for i, source in enumerate((left, far, right)):
        copy(wog.at[source], wog.at[source], o_send.at[i], o_recv.at[i], (kf, source)).wait_recv()
    for h in range(4):
        a_last(h)
    a_arrive(4)
    total = jnp.zeros((width, QW), jnp.float32)
    for g in range(n_x):
        total = total + jnp.dot(wog[g, :, 0:256], at[g, 0:256, :], preferred_element_type=jnp.float32)
    a_last(4)
    tail_w = jnp.concatenate([wog[g, :, 256:320] for g in range(n_x)], axis=1)
    tail_a = jnp.concatenate([at[g, 256:320, :] for g in range(n_x)], axis=0)
    total = total + jnp.dot(tail_w, tail_a, preferred_element_type=jnp.float32)
    total = total.astype(jnp.bfloat16)
    for f in range(2):
        out_ref[f] = total[:, f * PAD:(f + 1) * PAD]

    for f in range(2):
        for c in x_own(f) + x_fwd(f):
            c.wait_send()
        for part in pieces(f):
            for route in range(3):
                for c in kv_copies(f, part, route):
                    c.wait_send()
    for h in range(5):
        for c in a_own(h) + a_fwd(h):
            c.wait_send()
    for c in o_copies():
        c.wait_send()


def blend(base, ko_ref, next_ref, key_ref, tok_ref, num_ref, *rest):
    out_ref = rest[-1]
    j = pl.program_id(0)
    first_key = 2 * lax.axis_index("kf") + base
    rows = (key_ref[0] - first_key) * PAD + tok_ref[0]
    share = num_ref[pl.ds(base * 7 + j, 1), :].astype(jnp.float32) / DEN
    spot = lax.broadcasted_iota(jnp.int32, (2 * PAD, TOK), 0)
    pick = jnp.where(spot == rows[0:1], share, 0.0) + jnp.where(spot == rows[1:2], 1.0 - share, 0.0)
    window = jnp.concatenate([ko_ref[base], next_ref[0] if base else ko_ref[1]], axis=1)
    mixed = jnp.dot(window, pick.astype(jnp.bfloat16), preferred_element_type=jnp.float32)
    out_ref[0] = mixed.astype(jnp.bfloat16)


def blend_first(*refs):
    ko_ref, key_out = refs[0], refs[-2]

    @pl.when(pl.program_id(0) == 0)
    def _():
        key_out[...] = ko_ref[:, :, 0:TOK]

    blend(0, ko_ref, None, *refs[1:-2], refs[-1])


def body(key_states, w_query, w_key, w_value, w_out, gain, bias, src_key, src_tok, weight_num):
    n_x = lax.axis_size("head")
    frames, tokens, width = key_states.shape
    full = gain.shape[0]
    vmem = pl.BlockSpec(memory_space=pltpu.VMEM)
    anywhere = pl.BlockSpec(memory_space=pl.ANY)
    bf16, f32 = jnp.bfloat16, jnp.float32
    dma = pltpu.SemaphoreType.DMA
    ko = pl.pallas_call(
        functools.partial(attend, n_x),
        out_shape=jax.ShapeDtypeStruct((2, width, PAD), bf16),
        in_specs=[vmem, anywhere, anywhere, anywhere, anywhere, vmem, vmem],
        out_specs=vmem,
        scratch_shapes=[
            pltpu.VMEM((width, full), bf16), pltpu.VMEM((width, full), bf16), pltpu.VMEM((width, full), bf16),
            pltpu.VMEM((width, full), bf16),
            pltpu.VMEM((2, full, PAD), bf16),
            pltpu.VMEM((full, PAD), bf16),
            pltpu.VMEM((6, 128, QW), bf16),
            pltpu.VMEM((4, 2, 1280, 128), bf16),
            pltpu.VMEM((4, 2, width, PAD), bf16),
            pltpu.VMEM((2, 16, QW), bf16),
            pltpu.VMEM((5, 80, QW), f32),
            pltpu.VMEM((5, 1, QW), f32),
            pltpu.VMEM((4, width, QW), bf16),
            pltpu.VMEM((4, width, width), bf16),
            pltpu.VMEM((4, width, width), bf16),
            pltpu.VMEM((full, 2), f32),
            dma((4,)), dma((2, 4)), dma((2, 4)), dma((3, 4, 2)), dma((3, 4, 2)),
            dma((5, 4)), dma((5, 4)), dma((3,)), dma((3,)),
        ],
        compiler_params=pltpu.CompilerParams(
            collective_id=0, has_side_effects=True, vmem_limit_bytes=52 * 2**20),
        name="attend",
    )(key_states.transpose(0, 2, 1), w_query.T, w_key.T, w_value.T, w_out,
      gain.reshape(1, full), bias.reshape(1, full))
    n_kf = lax.axis_size("kf")
    following = lax.ppermute(ko[:1], "kf", [(i, i - 1) for i in range(1, n_kf)])

    keys_t, toks_t = src_key.transpose(0, 2, 1), src_tok.transpose(0, 2, 1)
    out = jax.ShapeDtypeStruct((14, width, TOK), bf16)
    cost = pl.CostEstimate(flops=2 * 7 * 320 * 1024 * 512, bytes_accessed=4_000_000, transcendentals=0)

    def index_spec(base):
        return pl.BlockSpec((1, 2, TOK), lambda j: (j + 7 * base, 0, 0))

    def whole(shape):
        return pl.BlockSpec(shape, lambda j: (0,) * len(shape))

    def out_spec(base):
        return pl.BlockSpec((1, width, TOK), lambda j: (j + 7 * base, 0, 0))

    params = pltpu.CompilerParams(vmem_limit_bytes=40 * 2**20)
    key_out, half_done = pl.pallas_call(
        blend_first,
        grid=(7,),
        out_shape=(jax.ShapeDtypeStruct((2, width, TOK), bf16), out),
        in_specs=[whole((2, width, PAD)), index_spec(0), index_spec(0), whole((14, TOK))],
        out_specs=(whole((2, width, TOK)), out_spec(0)),
        compiler_params=params, cost_estimate=cost, name="blend_first",
    )(ko, keys_t, toks_t, weight_num)
    blended = pl.pallas_call(
        functools.partial(blend, 1),
        grid=(7,),
        out_shape=out,
        in_specs=[whole((2, width, PAD)), whole((1, width, PAD)), index_spec(1), index_spec(1), whole((14, TOK)), anywhere],
        out_specs=out_spec(1),
        input_output_aliases={5: 0},
        compiler_params=params, cost_estimate=cost, name="blend_second",
    )(ko, following, keys_t, toks_t, weight_num, half_done)
    return key_out.transpose(0, 2, 1), blended.transpose(0, 2, 1)


def solution(mesh):
    return jax.shard_map(
        body,
        mesh=mesh,
        in_specs=(
            P("kf", None, "head"),
            P(None, "head"),
            P(None, "head"),
            P(None, "head"),
            P("head", None),
            P(),
            P(),
            P("kf", None, None),
            P("kf", None, None),
            P("kf", None),
        ),
        out_specs=(P("kf", None, "head"), P("kf", None, "head")),
        check_vma=False,
    )
```

```python
import functools

import jax
import jax.numpy as jnp
from jax import lax
from jax.experimental import pallas as pl
from jax.experimental.pallas import tpu as pltpu
from jax.sharding import PartitionSpec as P

MESH = pl.DeviceIdType.MESH
HD = 64
DEN = 16
TOK = 510
PAD = 512
QW = 2 * PAD
SCORE_SCALE = 0.125 * 1.4426950408889634
LOWEST = -3e38


def attend(n_x, x_hbm, wq_hbm, wk_hbm, wv_hbm, wo_hbm, gain_ref, bias_ref, out_ref, first_ref,
           xs, wq, wk, wv, wo, xg, nt, qz, kb, vb, ones, acc, top, at, wt, wog, gb,
           in_sem, x_send, x_recv, kv_send, kv_recv, a_send, a_recv, o_send, o_recv):
    kf = lax.axis_index("kf")
    x = lax.axis_index("head")
    right, left, far = lax.rem(x + 1, n_x), lax.rem(x + 3, n_x), lax.rem(x + 2, n_x)
    core = kf + 1 - 2 * lax.rem(kf, 2)
    ymate = kf + 2 - 4 * lax.rem(kf // 2, 2)
    dev_r, dev_l, dev_far, dev_core, dev_y = (kf, right), (kf, left), (kf, far), (core, x), (ymate, x)
    width = xs.shape[1]
    half_w = width // 2

    def copy(src, dst, send, recv, dev):
        return pltpu.make_async_remote_copy(
            src_ref=src, dst_ref=dst, send_sem=send, recv_sem=recv, device_id=dev, device_id_type=MESH)

    barrier = pltpu.get_barrier_semaphore()
    for dev in (dev_r, dev_l, dev_far, dev_core, dev_y):
        pl.semaphore_signal(barrier, inc=1, device_id=dev, device_id_type=MESH)

    loads = [pltpu.make_async_copy(a, b, in_sem.at[i])
             for i, (a, b) in enumerate(((x_hbm, xs), (wo_hbm, wo), (wk_hbm, wk), (wv_hbm, wv), (wq_hbm, wq)))]
    for load in loads:
        load.start()

    def ring(piece, sends, recvs):
        def one(owner, part, i, dev):
            return copy(piece(owner, part), piece(owner, part), sends(i), recvs(i), dev)

        def begin():
            for part, i in ((0, 0), (1, 1)):
                one(x, part, i, dev_r).start()
                one(x, 1 - part, 2 + i, dev_l).start()

        def relay():
            one(left, 0, 0, dev_l).wait_recv()
            one(left, 0, 4, dev_r).start()
            one(right, 1, 2, dev_r).wait_recv()
            one(right, 1, 5, dev_l).start()

        def near():
            one(left, 1, 1, dev_l).wait_recv()
            one(right, 0, 3, dev_r).wait_recv()

        def last():
            one(far, 0, 4, dev_l).wait_recv()
            one(far, 1, 5, dev_r).wait_recv()

        def drain():
            for part, i in ((0, 0), (1, 1)):
                one(x, part, i, dev_r).wait_send()
                one(x, 1 - part, 2 + i, dev_l).wait_send()
            one(left, 0, 4, dev_r).wait_send()
            one(right, 1, 5, dev_l).wait_send()

        return begin, relay, near, last, drain

    def x_piece(f):
        def piece(owner, part):
            return xg.at[f, pl.ds(pl.multiple_of(owner * width + part * half_w, 32), half_w)]

        return ring(piece, lambda i: x_send.at[f, i], lambda i: x_recv.at[f, i])

    x_begin, x_relay, x_near, x_last, x_drain = zip(x_piece(0), x_piece(1))

    loads[0].wait()
    own_rows = pl.ds(pl.multiple_of(x * width, 64), width)
    for f in range(2):
        xg[f, own_rows, pl.ds(PAD - 128, 128)] = jnp.zeros((width, 128), jnp.bfloat16)
        xg[f, own_rows, pl.ds(0, TOK)] = xs[f]
    pl.semaphore_wait(barrier, 5)
    x_begin[0]()

    n_tiles = gain_ref.shape[0]
    for i, ref in enumerate((gain_ref, bias_ref)):
        turned = jnp.concatenate([ref[...], jnp.zeros((16 - n_tiles, 128), jnp.float32)], axis=0).T
        for tile in range(n_tiles):
            gb[i, tile * 128:(tile + 1) * 128, :] = jnp.broadcast_to(turned[:, tile:tile + 1], (128, 128))
    qz[...] = jnp.zeros_like(qz)
    row = lax.broadcasted_iota(jnp.int32, ones.shape[1:], 0)
    col = lax.broadcasted_iota(jnp.int32, ones.shape[1:], 1)
    ones[0] = jnp.where((row == 0) & (col % PAD < TOK), 1.0, 0.0).astype(jnp.bfloat16)
    ones[1] = jnp.where(row == 0, 1.0, 0.0).astype(jnp.bfloat16)
    ones[2] = jnp.where((row == 0) & (col % 256 < 254), 1.0, 0.0).astype(jnp.bfloat16)
    loads[1].wait()
    for j in range(n_x):
        part = wo[:, j * width:(j + 1) * width].astype(jnp.float32)
        wt[j] = part.T.astype(jnp.bfloat16)
    wog[x] = wt[x]
    for load in loads[2:]:
        load.wait()

    def project(f):
        for i in range(PAD // 128):
            cols = pl.ds(i * 128, 128)
            values = xg[f, :, cols].astype(jnp.float32)
            center = jnp.mean(values, axis=0, keepdims=True)
            off = values - center
            spread = jnp.mean(off * off, axis=0, keepdims=True)
            nt[:, cols] = (off * lax.rsqrt(spread + 1e-05) * gb[0] + gb[1]).astype(jnp.bfloat16)

        lane = lax.broadcasted_iota(jnp.int32, (width, PAD), 1)
        k = jnp.dot(wk[...], nt[...], preferred_element_type=jnp.float32)
        k = jnp.where(lane < TOK, k, k[:, TOK - 1:TOK]).T.astype(jnp.bfloat16)
        kb[0, f, 0:512, :] = k[:, 0:128]
        kb[0, f, 512:1024, :] = k[:, 128:256]
        kb[0, f, 1024:1280, :] = jnp.concatenate([k[0:256, 256:320], k[256:512, 256:320]], axis=1)
        v = jnp.dot(wv[...], nt[...], preferred_element_type=jnp.float32)
        vb[0, f] = jnp.where(lane < TOK, v, 0.0).astype(jnp.bfloat16)
        for part in pieces(f):
            for c in kv_copies(f, part, 0):
                c.start()
        kv_to_y(f, pieces(f)[0])
        q = (jnp.dot(wq[...], nt[...], preferred_element_type=jnp.float32) * SCORE_SCALE).astype(jnp.bfloat16)
        for h in range(5):
            half = (h % 2) * HD
            qz[f, h, half:half + HD, :] = q[h * HD:(h + 1) * HD]
        qz[f, 5, HD:2 * HD, :] = q[4 * HD:5 * HD]

    def pieces(f):
        return (3,) if f == 0 else (0, 1, 2)

    def kv_rows(part):
        if isinstance(part, int):
            return ((pl.ds(0, 1280), pl.ds(0, 320)) if part == 3 else
                    (pl.ds(1024, 256), pl.ds(256, 64)) if part == 2 else
                    (pl.ds(part * 512, 512), pl.ds(part * 128, 128)))
        return pl.ds(pl.multiple_of(part * 512, 512), 512), pl.ds(pl.multiple_of(part * 128, 128), 128)

    def kv_copies(f, part, route, landed=False):
        k_rows, v_rows = kv_rows(part)
        source, target = (0, 0, 2)[route], (1, 2, 3)[route]
        source = target if landed else source
        dev = dev_y if route == 1 else dev_core
        return (copy(kb.at[source, f, k_rows], kb.at[target, f, k_rows],
                     kv_send.at[route, part, 0], kv_recv.at[route, part, 0], dev),
                copy(vb.at[source, f, v_rows], vb.at[target, f, v_rows],
                     kv_send.at[route, part, 1], kv_recv.at[route, part, 1], dev))

    def kv_to_y(f, part, behind=None):
        if behind is not None:
            for c in kv_copies(f, behind, 1):
                c.wait_send()
        for c in kv_copies(f, part, 1):
            c.start()

    def kv_wait(f, part, route):
        for c in kv_copies(f, part, route, landed=True):
            c.wait_recv()

    def kv_forward(f, part):
        kv_wait(f, part, 1)
        for c in kv_copies(f, part, 2):
            c.start()

    def update(qfs, h, s, values, first):
        m0 = jnp.concatenate([top[f, h] for f in qfs], axis=1) if not first else LOWEST
        m = jnp.maximum(m0, jnp.max(s, axis=0, keepdims=True))
        p = jnp.exp2(s - m).astype(jnp.bfloat16)
        term = jnp.dot(values, p, preferred_element_type=jnp.float32)
        for i, f in enumerate(qfs):
            cols = slice(i * PAD, (i + 1) * PAD)
            if first:
                acc[f, h] = term[:, cols]
            else:
                acc[f, h] = acc[f, h] * jnp.exp2(m0[:, cols] - m[:, cols]) + term[:, cols]
            top[f, h] = m[:, cols]

    def block(qfs, parts, h, first=False):
        rows = pl.ds(pl.multiple_of(h // 2 * 512, 512), 512)
        chans = pl.ds(pl.multiple_of(h * HD, HD), HD)
        keys = jnp.concatenate([kb[s, f, rows, :] for s, f in parts], axis=0)
        vals = jnp.concatenate([vb[s, f, chans, :] for s, f in parts], axis=1)
        q = jnp.concatenate([qz[f, h] for f in qfs], axis=1)
        s = jnp.dot(keys, q, preferred_element_type=jnp.float32)
        update(qfs, h, s, jnp.concatenate([vals, ones[0, :, 0:PAD * len(parts)]], axis=0), first)

    def block_last(qfs, parts, first=False):
        wide = 256 * len(parts)
        keys = jnp.concatenate([kb[s, f, 1024:1280, :] for s, f in parts], axis=0)
        vals = jnp.concatenate([vb[s, f, 256:320, 0:256] for s, f in parts]
                               + [vb[s, f, 256:320, 256:512] for s, f in parts], axis=1)
        q = [jnp.concatenate([qz[f, h] for f in qfs], axis=1) for h in (4, 5)]
        s = jnp.concatenate([jnp.dot(keys, t, preferred_element_type=jnp.float32) for t in q], axis=0)
        mask = jnp.concatenate([ones[1, :, 0:wide], ones[2, :, 0:wide]], axis=1)
        update(qfs, 4, s, jnp.concatenate([vals, mask], axis=0), first)

    def a_piece(n):
        def one(owner, part, i, dev):
            first, count = (0, HD) if part is None else (part * 32, 32)
            if not isinstance(n, int) or n < 4:
                piece = at.at[owner, :, pl.ds(pl.multiple_of(n * HD + first, 32), count)]
            else:
                piece = at.at[owner, n - 4, pl.ds(256 + first, count)]
            return copy(piece, piece, a_send.at[n, i], a_recv.at[n, i], dev)

        def begin():
            one(x, None, 0, dev_r).start()
            one(x, None, 1, dev_l).start()

        def relay():
            one(left, None, 0, dev_l).wait_recv()
            one(left, 0, 2, dev_r).start()
            one(right, None, 1, dev_r).wait_recv()
            one(right, 1, 3, dev_l).start()

        def last():
            one(far, 0, 2, dev_l).wait_recv()
            one(far, 1, 3, dev_r).wait_recv()

        def drain():
            one(x, None, 0, dev_r).wait_send()
            one(x, None, 1, dev_l).wait_send()
            one(left, 0, 2, dev_r).wait_send()
            one(right, 1, 3, dev_l).wait_send()

        return begin, relay, last, drain

    def finish(h, f):
        at[x, f, pl.ds(pl.multiple_of(h * HD, HD), HD), :] = (
            acc[f, h, 0:HD, :] / acc[f, h, HD:HD + 1, :]).astype(jnp.bfloat16)

    x_relay[0]()
    x_near[0]()
    x_last[0]()
    x_begin[1]()
    project(0)
    kv_wait(0, 3, 0)
    mine = ((0, 0), (1, 0))

    def early(h, _):
        block((0,), mine, h, True)
        return 0

    lax.fori_loop(0, 3, early, 0)
    x_relay[1]()
    lax.fori_loop(3, 4, early, 0)
    block_last((0,), mine, True)
    x_near[1]()
    x_last[1]()

    def o_copies():
        return [copy(wt.at[to], wog.at[x], o_send.at[i], o_recv.at[i], (kf, to))
                for i, to in enumerate((right, far, left))]

    for c in o_copies():
        c.start()
    project(1)

    def second(h, _):
        block((1,), mine, h, True)
        return 0

    lax.fori_loop(0, 2, second, 0)
    kv_forward(0, 3)
    lax.fori_loop(2, 4, second, 0)
    block_last((1,), mine, True)
    both = (0, 1)

    def near_block(h, _):
        block(both, ((0, 1), (1, 1), (2, 0), (3, 0)), h)
        return 0

    def far_block(h, relays):
        block(both, ((2, 1), (3, 1)), h)
        for n in relays:
            a_piece(n)[1]()
        for f in both:
            finish(h, f)
        a_piece(h)[0]()

    def first_far(h, _):
        far_block(h, ())
        return 0

    kv_wait(0, 3, 2)
    kv_wait(1, 0, 0)
    lax.fori_loop(0, 1, near_block, 0)
    kv_to_y(1, 1, 0)
    kv_forward(1, 0)
    lax.fori_loop(1, 2, near_block, 0)
    kv_to_y(1, 2, 1)
    kv_wait(1, 0, 2)
    lax.fori_loop(0, 2, first_far, 0)
    kv_wait(1, 1, 0)
    kv_forward(1, 1)

    def later(h, _):
        near_block(h, 0)

        @pl.when(h == 2)
        def _():
            a_piece(0)[1]()
            kv_wait(1, 1, 2)

        @pl.when(h == 3)
        def _():
            kv_forward(1, 2)

        far_block(h, (h - 1,))
        return 0

    lax.fori_loop(2, 4, later, 0)
    kv_wait(1, 2, 0)
    kv_wait(1, 2, 2)
    rest = ((0, 1), (1, 1), (2, 0), (3, 0), (2, 1), (3, 1))
    block_last((0,), rest)
    finish(4, 0)
    a_piece(4)[0]()
    block_last((1,), rest)
    a_piece(3)[1]()
    finish(4, 1)
    a_piece(5)[0]()

    def mix(f, first, count):
        w = jnp.concatenate([wog[g, :, first:first + count] for g in range(n_x)], axis=1)
        a = jnp.concatenate([at[g, f, first:first + count, :] for g in range(n_x)], axis=0)
        return jnp.dot(w, a, preferred_element_type=jnp.float32)

    for i, source in enumerate((left, far, right)):
        copy(wog.at[source], wog.at[source], o_send.at[i], o_recv.at[i], (kf, source)).wait_recv()
    a_piece(0)[2]()
    a_piece(1)[2]()
    total = [mix(f, 0, 128) for f in both]
    a_piece(4)[1]()
    a_piece(2)[2]()
    a_piece(5)[1]()
    a_piece(3)[2]()
    total = [total[f] + mix(f, 128, 128) for f in both]
    for f in both:
        a_piece(4 + f)[2]()
        out_ref[f] = (total[f] + mix(f, 256, 64)).astype(jnp.bfloat16)
        if f == 0:
            first_ref[0] = out_ref[0]

    for f in range(2):
        x_drain[f]()
        for part in pieces(f):
            for route in range(3):
                if route != 1 or part > 1:
                    for c in kv_copies(f, part, route):
                        c.wait_send()
    for n in range(6):
        a_piece(n)[3]()
    for c in o_copies():
        c.wait_send()


def blend(base, first_ref, second_ref, key_ref, tok_ref, num_ref, out_ref):
    each = out_ref.shape[0]
    first_key = 2 * lax.axis_index("kf") + base
    window = jnp.concatenate([first_ref[...], second_ref[...]], axis=1)
    spot = lax.broadcasted_iota(jnp.int16, (2 * PAD, TOK), 0)
    none = jnp.zeros((), jnp.bfloat16)
    for j in range(each):
        rows = ((key_ref[j] - first_key) * PAD + tok_ref[j]).astype(jnp.int16)
        share = num_ref[base * each + j:base * each + j + 1, :].astype(jnp.float32) / DEN
        pick = (jnp.where(spot == rows[0:1], share.astype(jnp.bfloat16), none)
                + jnp.where(spot == rows[1:2], (1.0 - share).astype(jnp.bfloat16), none))
        out_ref[j] = jnp.dot(window, pick, preferred_element_type=jnp.float32).astype(jnp.bfloat16)


def blend_first(ko_ref, key_ref, tok_ref, num_ref, key_out, out_ref):
    key_out[...] = ko_ref[:, :, 0:TOK]
    blend(0, ko_ref.at[0], ko_ref.at[1], key_ref, tok_ref, num_ref, out_ref)


def blend_second(ko_ref, next_ref, key_ref, tok_ref, num_ref, done_ref, out_ref):
    blend(1, ko_ref.at[1], next_ref.at[0], key_ref, tok_ref, num_ref, out_ref)


def body(key_states, w_query, w_key, w_value, w_out, gain, bias, src_key, src_tok, weight_num):
    n_x, n_kf = lax.axis_size("head"), lax.axis_size("kf")
    frames, tokens, width = key_states.shape
    full = gain.shape[0]
    vmem = pl.BlockSpec(memory_space=pltpu.VMEM)
    anywhere = pl.BlockSpec(memory_space=pltpu.HBM)
    bf16, f32 = jnp.bfloat16, jnp.float32
    dma = pltpu.SemaphoreType.DMA
    ko, ko_first = pl.pallas_call(
        functools.partial(attend, n_x),
        out_shape=(jax.ShapeDtypeStruct((2, width, PAD), bf16), jax.ShapeDtypeStruct((1, width, PAD), bf16)),
        in_specs=[anywhere] * 5 + [vmem, vmem],
        out_specs=(vmem, vmem),
        scratch_shapes=[
            pltpu.VMEM((frames, width, tokens), bf16),
            pltpu.VMEM((width, full), bf16), pltpu.VMEM((width, full), bf16), pltpu.VMEM((width, full), bf16),
            pltpu.VMEM((width, full), bf16),
            pltpu.VMEM((2, full, PAD), bf16),
            pltpu.VMEM((full, PAD), bf16),
            pltpu.VMEM((2, 6, 128, PAD), bf16),
            pltpu.VMEM((4, 2, 1280, 128), bf16),
            pltpu.VMEM((4, 2, width, PAD), bf16),
            pltpu.VMEM((3, 16, 6 * PAD), bf16),
            pltpu.VMEM((2, 5, 80, PAD), f32),
            pltpu.VMEM((2, 5, 1, PAD), f32),
            pltpu.VMEM((4, 2, width, PAD), bf16),
            pltpu.VMEM((4, width, width), bf16),
            pltpu.VMEM((4, width, width), bf16),
            pltpu.VMEM((2, full, 128), f32),
            dma((5,)), dma((2, 6)), dma((2, 6)), dma((3, 4, 2)), dma((3, 4, 2)),
            dma((6, 4)), dma((6, 4)), dma((3,)), dma((3,)),
        ],
        compiler_params=pltpu.CompilerParams(
            collective_id=0, has_side_effects=True, vmem_limit_bytes=56 * 2**20),
        name="attend",
    )(key_states.transpose(0, 2, 1), w_query.T, w_key.T, w_value.T, w_out,
      gain.reshape(full // 128, 128), bias.reshape(full // 128, 128))

    following = lax.ppermute(ko_first, "kf", [(i, i - 1) for i in range(1, n_kf)])

    def whole(shape):
        return pl.BlockSpec(shape, lambda j: (0,) * len(shape))

    n_out = weight_num.shape[0]
    each = n_out // frames
    keys_t, toks_t = src_key.transpose(0, 2, 1), src_tok.transpose(0, 2, 1)
    params = pltpu.CompilerParams(vmem_limit_bytes=40 * 2**20)
    cost = pl.CostEstimate(flops=2 * each * width * 2 * PAD * PAD, bytes_accessed=4_000_000, transcendentals=0)

    def part(base, shape):
        return pl.BlockSpec((each,) + shape, lambda j: (base, 0, 0))

    out = jax.ShapeDtypeStruct((n_out, width, tokens), bf16)
    key_out, half_done = pl.pallas_call(
        blend_first,
        grid=(1,),
        out_shape=(jax.ShapeDtypeStruct((frames, width, tokens), bf16), out),
        in_specs=[whole((2, width, PAD)), part(0, (2, tokens)), part(0, (2, tokens)), whole((n_out, tokens))],
        out_specs=(whole((frames, width, tokens)), part(0, (width, tokens))),
        compiler_params=params, cost_estimate=cost, name="blend_first",
    )(ko, keys_t, toks_t, weight_num)
    blended = pl.pallas_call(
        blend_second,
        grid=(1,),
        out_shape=out,
        in_specs=[whole((2, width, PAD)), whole((1, width, PAD)), part(1, (2, tokens)), part(1, (2, tokens)),
                  whole((n_out, tokens)), anywhere],
        out_specs=part(1, (width, tokens)),
        input_output_aliases={5: 0},
        compiler_params=params, cost_estimate=cost, name="blend_second",
    )(ko, following, keys_t, toks_t, weight_num, half_done)
    return key_out.transpose(0, 2, 1), blended.transpose(0, 2, 1)


def solution(mesh):
    return jax.shard_map(
        body,
        mesh=mesh,
        in_specs=(
            P("kf", None, "head"),
            P(None, "head"),
            P(None, "head"),
            P(None, "head"),
            P("head", None),
            P(),
            P(),
            P("kf", None, None),
            P("kf", None, None),
            P("kf", None),
        ),
        out_specs=(P("kf", None, "head"), P("kf", None, "head")),
        check_vma=False,
    )
```

```python
import functools

import jax
import jax.numpy as jnp
from jax import lax
from jax.experimental import pallas as pl
from jax.experimental.pallas import tpu as pltpu
from jax.sharding import PartitionSpec as P

MESH = pl.DeviceIdType.MESH
HD = 64
DEN = 16
TOK = 510
PAD = 512
QW = 2 * PAD
SCORE_SCALE = 0.125 * 1.4426950408889634
LOWEST = -3e38


def attend(n_x, x_hbm, wq_hbm, wk_hbm, wv_hbm, wo_hbm, gain_ref, bias_ref, out_ref, first_ref,
           xs, wq, wk, wv, wo, xg, nt, qz, kb, vb, ones, acc, top, at, wt, wog, gb,
           in_sem, x_send, x_recv, kv_send, kv_recv, a_send, a_recv, o_send, o_recv):
    kf = lax.axis_index("kf")
    x = lax.axis_index("head")
    right, left, far = lax.rem(x + 1, n_x), lax.rem(x + 3, n_x), lax.rem(x + 2, n_x)
    core = kf + 1 - 2 * lax.rem(kf, 2)
    ymate = kf + 2 - 4 * lax.rem(kf // 2, 2)
    dev_r, dev_l, dev_far, dev_core, dev_y = (kf, right), (kf, left), (kf, far), (core, x), (ymate, x)
    width = xs.shape[1]
    half_w = width // 2

    def copy(src, dst, send, recv, dev):
        return pltpu.make_async_remote_copy(
            src_ref=src, dst_ref=dst, send_sem=send, recv_sem=recv, device_id=dev, device_id_type=MESH)

    barrier = pltpu.get_barrier_semaphore()
    for dev in (dev_r, dev_l, dev_far, dev_core, dev_y):
        pl.semaphore_signal(barrier, inc=1, device_id=dev, device_id_type=MESH)

    loads = [pltpu.make_async_copy(a, b, in_sem.at[i])
             for i, (a, b) in enumerate(((x_hbm, xs), (wo_hbm, wo), (wk_hbm, wk), (wv_hbm, wv), (wq_hbm, wq)))]
    for load in loads:
        load.start()

    def ring(piece, sends, recvs):
        def one(owner, part, i, dev):
            return copy(piece(owner, part), piece(owner, part), sends(i), recvs(i), dev)

        def begin(halves=(0, 1)):
            for i in halves:
                one(x, i, i, dev_r).start()
                one(x, 1 - i, 2 + i, dev_l).start()

        def sent(i):
            if i < 2:
                one(x, i, i, dev_r).wait_send()
                one(x, 1 - i, 2 + i, dev_l).wait_send()
            else:
                one(left, 0, 4, dev_r).wait_send()
                one(right, 1, 5, dev_l).wait_send()

        def relay():
            one(left, 0, 0, dev_l).wait_recv()
            one(left, 0, 4, dev_r).start()
            one(right, 1, 2, dev_r).wait_recv()
            one(right, 1, 5, dev_l).start()

        def near():
            one(left, 1, 1, dev_l).wait_recv()
            one(right, 0, 3, dev_r).wait_recv()

        def last():
            one(far, 0, 4, dev_l).wait_recv()
            one(far, 1, 5, dev_r).wait_recv()

        return begin, relay, near, last, sent

    def x_piece(f):
        def piece(owner, part):
            return xg.at[f, pl.ds(pl.multiple_of(owner * width + part * half_w, 32), half_w)]

        return ring(piece, lambda i: x_send.at[f, i], lambda i: x_recv.at[f, i])

    x_begin, x_relay, x_near, x_last, x_sent = zip(x_piece(0), x_piece(1))

    loads[0].wait()
    own_rows = pl.ds(pl.multiple_of(x * width, 64), width)
    for f in range(2):
        xg[f, own_rows, pl.ds(PAD - 128, 128)] = jnp.zeros((width, 128), jnp.bfloat16)
        xg[f, own_rows, pl.ds(0, TOK)] = xs[f]
    pl.semaphore_wait(barrier, 5)
    x_begin[0]()

    n_tiles = gain_ref.shape[0]
    for i, ref in enumerate((gain_ref, bias_ref)):
        turned = jnp.concatenate([ref[...], jnp.zeros((16 - n_tiles, 128), jnp.float32)], axis=0).T
        for tile in range(n_tiles):
            gb[i, tile * 128:(tile + 1) * 128, :] = jnp.broadcast_to(turned[:, tile:tile + 1], (128, 128))
    qz[...] = jnp.zeros_like(qz)
    row = lax.broadcasted_iota(jnp.int32, ones.shape[1:], 0)
    col = lax.broadcasted_iota(jnp.int32, ones.shape[1:], 1)
    ones[0] = jnp.where((row == 0) & (col % PAD < TOK), 1.0, 0.0).astype(jnp.bfloat16)
    ones[1] = jnp.where(row == 0, 1.0, 0.0).astype(jnp.bfloat16)
    ones[2] = jnp.where((row == 0) & (col % 256 < 254), 1.0, 0.0).astype(jnp.bfloat16)
    loads[1].wait()
    for j in range(n_x):
        part = wo[:, j * width:(j + 1) * width].astype(jnp.float32)
        wt[j] = part.T.astype(jnp.bfloat16)
    wog[x] = wt[x]
    for load in loads[2:]:
        load.wait()

    def project(f):
        for i in range(PAD // 128):
            cols = pl.ds(i * 128, 128)
            values = xg[f, :, cols].astype(jnp.float32)
            center = jnp.mean(values, axis=0, keepdims=True)
            off = values - center
            spread = jnp.mean(off * off, axis=0, keepdims=True)
            nt[:, cols] = (off * lax.rsqrt(spread + 1e-05) * gb[0] + gb[1]).astype(jnp.bfloat16)

        lane = lax.broadcasted_iota(jnp.int32, (width, PAD), 1)
        k = jnp.dot(wk[...], nt[...], preferred_element_type=jnp.float32)
        k = jnp.where(lane < TOK, k, k[:, TOK - 1:TOK]).T.astype(jnp.bfloat16)
        kb[0, f, 0:512, :] = k[:, 0:128]
        kb[0, f, 512:1024, :] = k[:, 128:256]
        kb[0, f, 1024:1280, :] = jnp.concatenate([k[0:256, 256:320], k[256:512, 256:320]], axis=1)
        v = jnp.dot(wv[...], nt[...], preferred_element_type=jnp.float32)
        vb[0, f] = jnp.where(lane < TOK, v, 0.0).astype(jnp.bfloat16)
        for part in pieces(f):
            for c in kv_copies(f, part, 0):
                c.start()
        kv_to_y(f, pieces(f)[0])
        q = (jnp.dot(wq[...], nt[...], preferred_element_type=jnp.float32) * SCORE_SCALE).astype(jnp.bfloat16)
        for h in range(5):
            half = (h % 2) * HD
            qz[f, h, half:half + HD, :] = q[h * HD:(h + 1) * HD]
        qz[f, 5, HD:2 * HD, :] = q[4 * HD:5 * HD]

    def pieces(f):
        return (3,) if f == 0 else (0, 1, 2)

    def kv_rows(part):
        if isinstance(part, int):
            return ((pl.ds(0, 1280), pl.ds(0, 320)) if part == 3 else
                    (pl.ds(1024, 256), pl.ds(256, 64)) if part == 2 else
                    (pl.ds(part * 512, 512), pl.ds(part * 128, 128)))
        return pl.ds(pl.multiple_of(part * 512, 512), 512), pl.ds(pl.multiple_of(part * 128, 128), 128)

    def kv_copies(f, part, route, landed=False):
        k_rows, v_rows = kv_rows(part)
        source, target = (0, 0, 2)[route], (1, 2, 3)[route]
        source = target if landed else source
        dev = dev_y if route == 1 else dev_core
        return (copy(kb.at[source, f, k_rows], kb.at[target, f, k_rows],
                     kv_send.at[route, part, 0], kv_recv.at[route, part, 0], dev),
                copy(vb.at[source, f, v_rows], vb.at[target, f, v_rows],
                     kv_send.at[route, part, 1], kv_recv.at[route, part, 1], dev))

    def kv_to_y(f, part):
        for c in kv_copies(f, part, 1):
            c.start()

    def kv_wait(f, part, route):
        for c in kv_copies(f, part, route, landed=True):
            c.wait_recv()

    def kv_forward(f, part):
        kv_wait(f, part, 1)
        for c in kv_copies(f, part, 2):
            c.start()

    def update(qfs, h, s, values, first):
        m0 = jnp.concatenate([top[f, h] for f in qfs], axis=1) if not first else LOWEST
        m = jnp.maximum(m0, jnp.max(s, axis=0, keepdims=True))
        p = jnp.exp2(s - m).astype(jnp.bfloat16)
        term = jnp.dot(values, p, preferred_element_type=jnp.float32)
        for i, f in enumerate(qfs):
            cols = slice(i * PAD, (i + 1) * PAD)
            if first:
                acc[f, h] = term[:, cols]
            else:
                acc[f, h] = acc[f, h] * jnp.exp2(m0[:, cols] - m[:, cols]) + term[:, cols]
            top[f, h] = m[:, cols]

    def block(qfs, parts, h, first=False):
        rows = pl.ds(pl.multiple_of(h // 2 * 512, 512), 512)
        chans = pl.ds(pl.multiple_of(h * HD, HD), HD)
        keys = jnp.concatenate([kb[s, f, rows, :] for s, f in parts], axis=0)
        vals = jnp.concatenate([vb[s, f, chans, :] for s, f in parts], axis=1)
        q = jnp.concatenate([qz[f, h] for f in qfs], axis=1)
        s = jnp.dot(keys, q, preferred_element_type=jnp.float32)
        update(qfs, h, s, jnp.concatenate([vals, ones[0, :, 0:PAD * len(parts)]], axis=0), first)

    def block_last(qfs, parts, first=False):
        wide = 256 * len(parts)
        keys = jnp.concatenate([kb[s, f, 1024:1280, :] for s, f in parts], axis=0)
        vals = jnp.concatenate([vb[s, f, 256:320, 0:256] for s, f in parts]
                               + [vb[s, f, 256:320, 256:512] for s, f in parts], axis=1)
        q = [jnp.concatenate([qz[f, h] for f in qfs], axis=1) for h in (4, 5)]
        s = jnp.concatenate([jnp.dot(keys, t, preferred_element_type=jnp.float32) for t in q], axis=0)
        mask = jnp.concatenate([ones[1, :, 0:wide], ones[2, :, 0:wide]], axis=1)
        update(qfs, 4, s, jnp.concatenate([vals, mask], axis=0), first)

    def a_piece(n):
        def one(owner, part, i, dev):
            first, count = (0, HD) if part is None else (part * 32, 32)
            if not isinstance(n, int) or n < 4:
                piece = at.at[owner, :, pl.ds(pl.multiple_of(n * HD + first, 32), count)]
            else:
                piece = at.at[owner, n - 4, pl.ds(256 + first, count)]
            return copy(piece, piece, a_send.at[n, i], a_recv.at[n, i], dev)

        def begin():
            one(x, None, 0, dev_r).start()
            one(x, None, 1, dev_l).start()

        def relay():
            one(left, None, 0, dev_l).wait_recv()
            one(left, 0, 2, dev_r).start()
            one(right, None, 1, dev_r).wait_recv()
            one(right, 1, 3, dev_l).start()

        def last():
            one(far, 0, 2, dev_l).wait_recv()
            one(far, 1, 3, dev_r).wait_recv()

        def drain():
            one(x, None, 0, dev_r).wait_send()
            one(x, None, 1, dev_l).wait_send()
            one(left, 0, 2, dev_r).wait_send()
            one(right, 1, 3, dev_l).wait_send()

        return begin, relay, last, drain

    def finish(h, f):
        at[x, f, pl.ds(pl.multiple_of(h * HD, HD), HD), :] = (
            acc[f, h, 0:HD, :] / acc[f, h, HD:HD + 1, :]).astype(jnp.bfloat16)

    x_relay[0]()
    x_near[0]()
    x_sent[0](2)
    x_begin[1]()
    x_last[0]()
    project(0)
    kv_wait(0, 3, 0)
    mine = ((0, 0), (1, 0))

    def early(h, _):
        block((0,), mine, h, True)
        return 0

    lax.fori_loop(0, 3, early, 0)
    x_relay[1]()
    lax.fori_loop(3, 4, early, 0)
    block_last((0,), mine, True)
    x_near[1]()
    x_last[1]()

    def o_copies():
        return [copy(wt.at[to], wog.at[x], o_send.at[i], o_recv.at[i], (kf, to))
                for i, to in enumerate((right, far, left))]

    for c in o_copies():
        c.start()
    project(1)

    def second(h, _):
        block((1,), mine, h, True)
        return 0

    lax.fori_loop(0, 2, second, 0)
    kv_to_y(1, 1)
    kv_forward(0, 3)
    lax.fori_loop(2, 4, second, 0)
    block_last((1,), mine, True)
    both = (0, 1)

    def near_block(h, _):
        block(both, ((0, 1), (1, 1), (2, 0), (3, 0)), h)
        return 0

    def far_block(h, relays):
        block(both, ((2, 1), (3, 1)), h)
        for n in relays:
            a_piece(n)[1]()
        for f in both:
            finish(h, f)
        a_piece(h)[0]()

    def first_far(h, _):
        far_block(h, ())
        return 0

    kv_wait(0, 3, 2)
    kv_wait(1, 0, 0)
    lax.fori_loop(0, 1, near_block, 0)
    kv_to_y(1, 2)
    kv_forward(1, 0)
    lax.fori_loop(1, 2, near_block, 0)
    kv_wait(1, 0, 2)
    lax.fori_loop(0, 2, first_far, 0)
    kv_wait(1, 1, 0)
    kv_forward(1, 1)

    def later(h, _):
        near_block(h, 0)

        @pl.when(h == 2)
        def _():
            a_piece(0)[1]()
            kv_wait(1, 1, 2)

        @pl.when(h == 3)
        def _():
            kv_forward(1, 2)

        far_block(h, (h - 1,))
        return 0

    lax.fori_loop(2, 4, later, 0)
    kv_wait(1, 2, 0)
    kv_wait(1, 2, 2)
    rest = ((0, 1), (1, 1), (2, 0), (3, 0), (2, 1), (3, 1))
    block_last((0,), rest)
    finish(4, 0)
    a_piece(4)[0]()
    block_last((1,), rest)
    a_piece(3)[1]()
    finish(4, 1)
    a_piece(5)[0]()

    def mix(f, first, count):
        w = jnp.concatenate([wog[g, :, first:first + count] for g in range(n_x)], axis=1)
        a = jnp.concatenate([at[g, f, first:first + count, :] for g in range(n_x)], axis=0)
        return jnp.dot(w, a, preferred_element_type=jnp.float32)

    for i, source in enumerate((left, far, right)):
        copy(wog.at[source], wog.at[source], o_send.at[i], o_recv.at[i], (kf, source)).wait_recv()
    a_piece(0)[2]()
    a_piece(1)[2]()
    total = [mix(f, 0, 128) for f in both]
    a_piece(4)[1]()
    a_piece(2)[2]()
    a_piece(5)[1]()
    a_piece(3)[2]()
    total = [total[f] + mix(f, 128, 128) for f in both]
    for f in both:
        a_piece(4 + f)[2]()
        out_ref[f] = (total[f] + mix(f, 256, 64)).astype(jnp.bfloat16)
        if f == 0:
            first_ref[0] = out_ref[0]

    for f in range(2):
        for i in ((0, 1), (0, 1, 2))[f]:
            x_sent[f](i)
        for part in pieces(f):
            for route in range(3):
                for c in kv_copies(f, part, route):
                    c.wait_send()
    for n in range(6):
        a_piece(n)[3]()
    for c in o_copies():
        c.wait_send()


def blend(base, first_ref, second_ref, key_ref, tok_ref, num_ref, out_hbm, made, sems):
    each = made.shape[0]
    first_key = 2 * lax.axis_index("kf") + base
    window = jnp.concatenate([first_ref[...], second_ref[...]], axis=1)
    spot = lax.broadcasted_iota(jnp.int16, (2 * PAD, TOK), 0)
    none = jnp.zeros((), jnp.bfloat16)
    copies = [pltpu.make_async_copy(made.at[j], out_hbm.at[base * each + j], sems.at[j]) for j in range(each)]
    for j in range(each):
        rows = ((key_ref[j] - first_key) * PAD + tok_ref[j]).astype(jnp.int16)
        share = num_ref[base * each + j:base * each + j + 1, :].astype(jnp.float32) / DEN
        pick = (jnp.where(spot == rows[0:1], share.astype(jnp.bfloat16), none)
                + jnp.where(spot == rows[1:2], (1.0 - share).astype(jnp.bfloat16), none))
        made[j] = jnp.dot(window, pick, preferred_element_type=jnp.float32).astype(jnp.bfloat16)
        copies[j].start()
    for c in copies:
        c.wait()


def blend_first(ko_ref, key_ref, tok_ref, num_ref, key_out, out_hbm, made, sems):
    key_out[...] = ko_ref[:, :, 0:TOK]
    blend(0, ko_ref.at[0], ko_ref.at[1], key_ref, tok_ref, num_ref, out_hbm, made, sems)


def blend_second(ko_ref, next_ref, key_ref, tok_ref, num_ref, done_ref, out_hbm, made, sems):
    blend(1, ko_ref.at[1], next_ref.at[0], key_ref, tok_ref, num_ref, out_hbm, made, sems)


def body(key_states, w_query, w_key, w_value, w_out, gain, bias, src_key, src_tok, weight_num):
    n_x, n_kf = lax.axis_size("head"), lax.axis_size("kf")
    frames, tokens, width = key_states.shape
    full = gain.shape[0]
    vmem = pl.BlockSpec(memory_space=pltpu.VMEM)
    anywhere = pl.BlockSpec(memory_space=pltpu.HBM)
    bf16, f32 = jnp.bfloat16, jnp.float32
    dma = pltpu.SemaphoreType.DMA
    ko, ko_first = pl.pallas_call(
        functools.partial(attend, n_x),
        out_shape=(jax.ShapeDtypeStruct((2, width, PAD), bf16), jax.ShapeDtypeStruct((1, width, PAD), bf16)),
        in_specs=[anywhere] * 5 + [vmem, vmem],
        out_specs=(vmem, vmem),
        scratch_shapes=[
            pltpu.VMEM((frames, width, tokens), bf16),
            pltpu.VMEM((width, full), bf16), pltpu.VMEM((width, full), bf16), pltpu.VMEM((width, full), bf16),
            pltpu.VMEM((width, full), bf16),
            pltpu.VMEM((2, full, PAD), bf16),
            pltpu.VMEM((full, PAD), bf16),
            pltpu.VMEM((2, 6, 128, PAD), bf16),
            pltpu.VMEM((4, 2, 1280, 128), bf16),
            pltpu.VMEM((4, 2, width, PAD), bf16),
            pltpu.VMEM((3, 16, 6 * PAD), bf16),
            pltpu.VMEM((2, 5, 80, PAD), f32),
            pltpu.VMEM((2, 5, 1, PAD), f32),
            pltpu.VMEM((4, 2, width, PAD), bf16),
            pltpu.VMEM((4, width, width), bf16),
            pltpu.VMEM((4, width, width), bf16),
            pltpu.VMEM((2, full, 128), f32),
            dma((5,)), dma((2, 6)), dma((2, 6)), dma((3, 4, 2)), dma((3, 4, 2)),
            dma((6, 4)), dma((6, 4)), dma((3,)), dma((3,)),
        ],
        compiler_params=pltpu.CompilerParams(
            collective_id=0, has_side_effects=True, vmem_limit_bytes=56 * 2**20),
        name="attend",
    )(key_states.transpose(0, 2, 1), w_query.T, w_key.T, w_value.T, w_out,
      gain.reshape(full // 128, 128), bias.reshape(full // 128, 128))

    following = lax.ppermute(ko_first, "kf", [(i, i - 1) for i in range(1, n_kf)])

    def whole(shape):
        return pl.BlockSpec(shape, lambda j: (0,) * len(shape))

    n_out = weight_num.shape[0]
    each = n_out // frames
    keys_t, toks_t = src_key.transpose(0, 2, 1), src_tok.transpose(0, 2, 1)
    params = pltpu.CompilerParams(vmem_limit_bytes=40 * 2**20)
    cost = pl.CostEstimate(flops=2 * each * width * 2 * PAD * PAD, bytes_accessed=4_000_000, transcendentals=0)

    def part(base, shape):
        return pl.BlockSpec((each,) + shape, lambda j: (base, 0, 0))

    out = jax.ShapeDtypeStruct((n_out, width, tokens), bf16)
    made = [pltpu.VMEM((each, width, tokens), bf16), dma((each,))]
    key_out, half_done = pl.pallas_call(
        blend_first,
        grid=(1,),
        out_shape=(jax.ShapeDtypeStruct((frames, width, tokens), bf16), out),
        in_specs=[whole((2, width, PAD)), part(0, (2, tokens)), part(0, (2, tokens)), whole((n_out, tokens))],
        out_specs=(whole((frames, width, tokens)), anywhere),
        scratch_shapes=made,
        compiler_params=params, cost_estimate=cost, name="blend_first",
    )(ko, keys_t, toks_t, weight_num)
    blended = pl.pallas_call(
        blend_second,
        grid=(1,),
        out_shape=out,
        in_specs=[whole((2, width, PAD)), whole((1, width, PAD)), part(1, (2, tokens)), part(1, (2, tokens)),
                  whole((n_out, tokens)), anywhere],
        out_specs=anywhere,
        scratch_shapes=made,
        input_output_aliases={5: 0},
        compiler_params=params, cost_estimate=cost, name="blend_second",
    )(ko, following, keys_t, toks_t, weight_num, half_done)
    return key_out.transpose(0, 2, 1), blended.transpose(0, 2, 1)


def solution(mesh):
    return jax.shard_map(
        body,
        mesh=mesh,
        in_specs=(
            P("kf", None, "head"),
            P(None, "head"),
            P(None, "head"),
            P(None, "head"),
            P("head", None),
            P(),
            P(),
            P("kf", None, None),
            P("kf", None, None),
            P("kf", None),
        ),
        out_specs=(P("kf", None, "head"), P("kf", None, "head")),
        check_vma=False,
    )
```

```python
import functools

import jax
import jax.numpy as jnp
from jax import lax
from jax.experimental import pallas as pl
from jax.experimental.pallas import tpu as pltpu
from jax.sharding import PartitionSpec as P

MESH = pl.DeviceIdType.MESH
HD = 64
DEN = 16
TOK = 510
PAD = 512
QW = 2 * PAD
SCORE_SCALE = 0.125 * 1.4426950408889634
LOWEST = -3e38


def attend(n_x, x_hbm, wq_hbm, wk_hbm, wv_hbm, wo_hbm, gain_ref, bias_ref, out_ref, first_ref,
           xs, wq, wk, wv, wo, xg, nt, qz, kb, vb, ones, acc, top, at, wt, wog, gb,
           in_sem, x_send, x_recv, kv_send, kv_recv, a_send, a_recv, o_send, o_recv):
    kf = lax.axis_index("kf")
    x = lax.axis_index("head")
    right, left, far = lax.rem(x + 1, n_x), lax.rem(x + 3, n_x), lax.rem(x + 2, n_x)
    core = kf + 1 - 2 * lax.rem(kf, 2)
    ymate = kf + 2 - 4 * lax.rem(kf // 2, 2)
    dev_r, dev_l, dev_far, dev_core, dev_y = (kf, right), (kf, left), (kf, far), (core, x), (ymate, x)
    width = xs.shape[1]
    half_w = width // 2

    def copy(src, dst, send, recv, dev):
        return pltpu.make_async_remote_copy(
            src_ref=src, dst_ref=dst, send_sem=send, recv_sem=recv, device_id=dev, device_id_type=MESH)

    barrier = pltpu.get_barrier_semaphore()
    for dev in (dev_r, dev_l, dev_far, dev_core, dev_y):
        pl.semaphore_signal(barrier, inc=1, device_id=dev, device_id_type=MESH)

    loads = [pltpu.make_async_copy(a, b, in_sem.at[i])
             for i, (a, b) in enumerate(((x_hbm, xs), (wo_hbm, wo), (wk_hbm, wk), (wv_hbm, wv), (wq_hbm, wq)))]
    for load in loads:
        load.start()

    def ring(piece, sends, recvs):
        def one(owner, part, i, dev):
            return copy(piece(owner, part), piece(owner, part), sends(i), recvs(i), dev)

        def begin(halves=(0, 1)):
            for i in halves:
                one(x, i, i, dev_r).start()
                one(x, 1 - i, 2 + i, dev_l).start()

        def sent(i):
            if i < 2:
                one(x, i, i, dev_r).wait_send()
                one(x, 1 - i, 2 + i, dev_l).wait_send()
            else:
                one(left, 0, 4, dev_r).wait_send()
                one(right, 1, 5, dev_l).wait_send()

        def relay():
            one(left, 0, 0, dev_l).wait_recv()
            one(left, 0, 4, dev_r).start()
            one(right, 1, 2, dev_r).wait_recv()
            one(right, 1, 5, dev_l).start()

        def near():
            one(left, 1, 1, dev_l).wait_recv()
            one(right, 0, 3, dev_r).wait_recv()

        def last():
            one(far, 0, 4, dev_l).wait_recv()
            one(far, 1, 5, dev_r).wait_recv()

        return begin, relay, near, last, sent

    def x_piece(f):
        def piece(owner, part):
            return xg.at[f, pl.ds(pl.multiple_of(owner * width + part * half_w, 32), half_w)]

        return ring(piece, lambda i: x_send.at[f, i], lambda i: x_recv.at[f, i])

    x_begin, x_relay, x_near, x_last, x_sent = zip(x_piece(0), x_piece(1))

    loads[0].wait()
    own_rows = pl.ds(pl.multiple_of(x * width, 64), width)
    for f in range(2):
        xg[f, own_rows, pl.ds(PAD - 128, 128)] = jnp.zeros((width, 128), jnp.bfloat16)
        xg[f, own_rows, pl.ds(0, TOK)] = xs[f]
    pl.semaphore_wait(barrier, 5)
    x_begin[0]()

    n_tiles = gain_ref.shape[0]
    for i, ref in enumerate((gain_ref, bias_ref)):
        turned = jnp.concatenate([ref[...], jnp.zeros((16 - n_tiles, 128), jnp.float32)], axis=0).T
        for tile in range(n_tiles):
            gb[i, tile * 128:(tile + 1) * 128, :] = jnp.broadcast_to(turned[:, tile:tile + 1], (128, 128))
    qz[...] = jnp.zeros_like(qz)
    row = lax.broadcasted_iota(jnp.int32, ones.shape[1:], 0)
    col = lax.broadcasted_iota(jnp.int32, ones.shape[1:], 1)
    ones[0] = jnp.where((row == 0) & (col % PAD < TOK), 1.0, 0.0).astype(jnp.bfloat16)
    ones[1] = jnp.where(row == 0, 1.0, 0.0).astype(jnp.bfloat16)
    ones[2] = jnp.where((row == 0) & (col % 256 < 254), 1.0, 0.0).astype(jnp.bfloat16)
    loads[1].wait()
    for j in range(n_x):
        part = wo[:, j * width:(j + 1) * width].astype(jnp.float32)
        wt[j] = part.T.astype(jnp.bfloat16)
    wog[x] = wt[x]
    for load in loads[2:]:
        load.wait()

    def project(f):
        for i in range(PAD // 128):
            cols = pl.ds(i * 128, 128)
            values = xg[f, :, cols].astype(jnp.float32)
            center = jnp.mean(values, axis=0, keepdims=True)
            off = values - center
            spread = jnp.mean(off * off, axis=0, keepdims=True)
            nt[:, cols] = (off * lax.rsqrt(spread + 1e-05) * gb[0] + gb[1]).astype(jnp.bfloat16)

        lane = lax.broadcasted_iota(jnp.int32, (width, PAD), 1)
        k = jnp.dot(wk[...], nt[...], preferred_element_type=jnp.float32)
        k = jnp.where(lane < TOK, k, k[:, TOK - 1:TOK]).T.astype(jnp.bfloat16)
        kb[0, f, 0:512, :] = k[:, 0:128]
        kb[0, f, 512:1024, :] = k[:, 128:256]
        kb[0, f, 1024:1280, :] = jnp.concatenate([k[0:256, 256:320], k[256:512, 256:320]], axis=1)
        v = jnp.dot(wv[...], nt[...], preferred_element_type=jnp.float32)
        vb[0, f] = jnp.where(lane < TOK, v, 0.0).astype(jnp.bfloat16)
        for part in pieces(f):
            for c in kv_copies(f, part, 0):
                c.start()
        kv_to_y(f, pieces(f)[0])
        q = (jnp.dot(wq[...], nt[...], preferred_element_type=jnp.float32) * SCORE_SCALE).astype(jnp.bfloat16)
        for h in range(5):
            half = (h % 2) * HD
            qz[f, h, half:half + HD, :] = q[h * HD:(h + 1) * HD]
        qz[f, 5, HD:2 * HD, :] = q[4 * HD:5 * HD]

    def pieces(f):
        return (3,) if f == 0 else (0, 1, 2)

    def kv_rows(part):
        if isinstance(part, int):
            return ((pl.ds(0, 1280), pl.ds(0, 320)) if part == 3 else
                    (pl.ds(1024, 256), pl.ds(256, 64)) if part == 2 else
                    (pl.ds(part * 512, 512), pl.ds(part * 128, 128)))
        return pl.ds(pl.multiple_of(part * 512, 512), 512), pl.ds(pl.multiple_of(part * 128, 128), 128)

    def kv_copies(f, part, route, landed=False):
        k_rows, v_rows = kv_rows(part)
        source, target = (0, 0, 2)[route], (1, 2, 3)[route]
        source = target if landed else source
        dev = dev_y if route == 1 else dev_core
        return (copy(kb.at[source, f, k_rows], kb.at[target, f, k_rows],
                     kv_send.at[route, part, 0], kv_recv.at[route, part, 0], dev),
                copy(vb.at[source, f, v_rows], vb.at[target, f, v_rows],
                     kv_send.at[route, part, 1], kv_recv.at[route, part, 1], dev))

    def kv_to_y(f, part):
        for c in kv_copies(f, part, 1):
            c.start()

    def kv_wait(f, part, route):
        for c in kv_copies(f, part, route, landed=True):
            c.wait_recv()

    def kv_forward(f, part):
        kv_wait(f, part, 1)
        for c in kv_copies(f, part, 2):
            c.start()

    def update(qfs, h, s, values, first):
        m0 = jnp.concatenate([top[f, h] for f in qfs], axis=1) if not first else LOWEST
        m = jnp.maximum(m0, jnp.max(s, axis=0, keepdims=True))
        p = jnp.exp2(s - m).astype(jnp.bfloat16)
        term = jnp.dot(values, p, preferred_element_type=jnp.float32)
        for i, f in enumerate(qfs):
            cols = slice(i * PAD, (i + 1) * PAD)
            if first:
                acc[f, h] = term[:, cols]
            else:
                acc[f, h] = acc[f, h] * jnp.exp2(m0[:, cols] - m[:, cols]) + term[:, cols]
            top[f, h] = m[:, cols]

    def block(qfs, parts, h, first=False):
        rows = pl.ds(pl.multiple_of(h // 2 * 512, 512), 512)
        chans = pl.ds(pl.multiple_of(h * HD, HD), HD)
        keys = jnp.concatenate([kb[s, f, rows, :] for s, f in parts], axis=0)
        vals = jnp.concatenate([vb[s, f, chans, :] for s, f in parts], axis=1)
        q = jnp.concatenate([qz[f, h] for f in qfs], axis=1)
        s = jnp.dot(keys, q, preferred_element_type=jnp.float32)
        update(qfs, h, s, jnp.concatenate([vals, ones[0, :, 0:PAD * len(parts)]], axis=0), first)

    def block_last(qfs, parts, first=False):
        wide = 256 * len(parts)
        keys = jnp.concatenate([kb[s, f, 1024:1280, :] for s, f in parts], axis=0)
        vals = jnp.concatenate([vb[s, f, 256:320, 0:256] for s, f in parts]
                               + [vb[s, f, 256:320, 256:512] for s, f in parts], axis=1)
        q = [jnp.concatenate([qz[f, h] for f in qfs], axis=1) for h in (4, 5)]
        s = jnp.concatenate([jnp.dot(keys, t, preferred_element_type=jnp.float32) for t in q], axis=0)
        mask = jnp.concatenate([ones[1, :, 0:wide], ones[2, :, 0:wide]], axis=1)
        update(qfs, 4, s, jnp.concatenate([vals, mask], axis=0), first)

    def a_piece(n):
        def one(owner, part, i, dev):
            first, count = (0, HD) if part is None else (part * 32, 32)
            if not isinstance(n, int) or n < 4:
                piece = at.at[owner, :, pl.ds(pl.multiple_of(n * HD + first, 32), count)]
            else:
                piece = at.at[owner, n - 4, pl.ds(256 + first, count)]
            return copy(piece, piece, a_send.at[n, i], a_recv.at[n, i], dev)

        def begin():
            one(x, None, 0, dev_r).start()
            one(x, None, 1, dev_l).start()

        def relay():
            one(left, None, 0, dev_l).wait_recv()
            one(left, 0, 2, dev_r).start()
            one(right, None, 1, dev_r).wait_recv()
            one(right, 1, 3, dev_l).start()

        def last():
            one(far, 0, 2, dev_l).wait_recv()
            one(far, 1, 3, dev_r).wait_recv()

        def drain():
            one(x, None, 0, dev_r).wait_send()
            one(x, None, 1, dev_l).wait_send()
            one(left, 0, 2, dev_r).wait_send()
            one(right, 1, 3, dev_l).wait_send()

        return begin, relay, last, drain

    def finish(h, f):
        at[x, f, pl.ds(pl.multiple_of(h * HD, HD), HD), :] = (
            acc[f, h, 0:HD, :] / acc[f, h, HD:HD + 1, :]).astype(jnp.bfloat16)

    x_relay[0]()
    x_near[0]()
    x_sent[0](2)
    x_begin[1]()
    x_last[0]()
    project(0)
    kv_wait(0, 3, 0)
    mine = ((0, 0), (1, 0))

    def early(h, _):
        block((0,), mine, h, True)
        return 0

    lax.fori_loop(0, 3, early, 0)
    x_relay[1]()
    lax.fori_loop(3, 4, early, 0)
    block_last((0,), mine, True)
    x_near[1]()
    x_last[1]()

    def o_copies():
        return [copy(wt.at[to], wog.at[x], o_send.at[i], o_recv.at[i], (kf, to))
                for i, to in enumerate((right, far, left))]

    for c in o_copies():
        c.start()
    project(1)

    def second(h, _):
        block((1,), mine, h, True)
        return 0

    lax.fori_loop(0, 2, second, 0)
    kv_to_y(1, 1)
    kv_forward(0, 3)
    lax.fori_loop(2, 4, second, 0)
    block_last((1,), mine, True)
    both = (0, 1)

    def near_block(h, _):
        block(both, ((0, 1), (1, 1), (2, 0), (3, 0)), h)
        return 0

    def far_block(h, relays):
        block(both, ((2, 1), (3, 1)), h)
        for n in relays:
            a_piece(n)[1]()
        for f in both:
            finish(h, f)
        a_piece(h)[0]()

    def first_far(h, _):
        far_block(h, ())
        return 0

    kv_wait(0, 3, 2)
    kv_wait(1, 0, 0)
    lax.fori_loop(0, 1, near_block, 0)
    kv_to_y(1, 2)
    kv_forward(1, 0)
    lax.fori_loop(1, 2, near_block, 0)
    kv_wait(1, 0, 2)
    lax.fori_loop(0, 2, first_far, 0)
    kv_wait(1, 1, 0)
    kv_forward(1, 1)

    def later(h, _):
        near_block(h, 0)

        @pl.when(h == 2)
        def _():
            a_piece(0)[1]()
            kv_wait(1, 1, 2)

        @pl.when(h == 3)
        def _():
            kv_forward(1, 2)

        far_block(h, (h - 1,))
        return 0

    lax.fori_loop(2, 4, later, 0)
    kv_wait(1, 2, 0)
    kv_wait(1, 2, 2)
    rest = ((0, 1), (1, 1), (2, 0), (3, 0), (2, 1), (3, 1))
    block_last((0,), rest)
    finish(4, 0)
    a_piece(4)[0]()
    block_last((1,), rest)
    a_piece(3)[1]()
    finish(4, 1)
    a_piece(5)[0]()

    def mix(f, first, count):
        w = jnp.concatenate([wog[g, :, first:first + count] for g in range(n_x)], axis=1)
        a = jnp.concatenate([at[g, f, first:first + count, :] for g in range(n_x)], axis=0)
        return jnp.dot(w, a, preferred_element_type=jnp.float32)

    for i, source in enumerate((left, far, right)):
        copy(wog.at[source], wog.at[source], o_send.at[i], o_recv.at[i], (kf, source)).wait_recv()
    a_piece(0)[2]()
    a_piece(1)[2]()
    total = [mix(f, 0, 128) for f in both]
    a_piece(4)[1]()
    a_piece(2)[2]()
    a_piece(5)[1]()
    a_piece(3)[2]()
    total = [total[f] + mix(f, 128, 128) for f in both]
    for f in both:
        a_piece(4 + f)[2]()
        out_ref[f] = (total[f] + mix(f, 256, 64)).astype(jnp.bfloat16)
        if f == 0:
            first_ref[0] = out_ref[0]

    for f in range(2):
        for i in ((0, 1), (0, 1, 2))[f]:
            x_sent[f](i)
        for part in pieces(f):
            for route in range(3):
                for c in kv_copies(f, part, route):
                    c.wait_send()
    for n in range(6):
        a_piece(n)[3]()
    for c in o_copies():
        c.wait_send()


def blend(base, first_ref, second_ref, key_ref, tok_ref, num_ref, out_hbm, made, sems):
    each = made.shape[0]
    first_key = 2 * lax.axis_index("kf") + base
    window = jnp.concatenate([first_ref[...], second_ref[...]], axis=1)
    spot = lax.broadcasted_iota(jnp.int16, (2 * PAD, TOK), 0)
    none = jnp.zeros((), jnp.bfloat16)
    copies = [pltpu.make_async_copy(made.at[j], out_hbm.at[base * each + j], sems.at[j]) for j in range(each)]
    for j in range(each):
        rows = ((key_ref[j] - first_key) * PAD + tok_ref[j]).astype(jnp.int16)
        share = num_ref[base * each + j:base * each + j + 1, :].astype(jnp.float32) / DEN
        pick = (jnp.where(spot == rows[0:1], share.astype(jnp.bfloat16), none)
                + jnp.where(spot == rows[1:2], (1.0 - share).astype(jnp.bfloat16), none))
        made[j] = jnp.dot(window, pick, preferred_element_type=jnp.float32).astype(jnp.bfloat16)
        copies[j].start()
    for c in copies:
        c.wait()


def blend_first(ko_ref, key_ref, tok_ref, num_ref, key_out, out_hbm, made, sems, cut, cut_sem):
    cut[...] = ko_ref[:, :, 0:TOK]
    leave = pltpu.make_async_copy(cut, key_out, cut_sem)
    leave.start()
    blend(0, ko_ref.at[0], ko_ref.at[1], key_ref, tok_ref, num_ref, out_hbm, made, sems)
    leave.wait()


def blend_second(ko_ref, next_ref, key_ref, tok_ref, num_ref, done_ref, out_hbm, made, sems):
    blend(1, ko_ref.at[1], next_ref.at[0], key_ref, tok_ref, num_ref, out_hbm, made, sems)


def body(key_states, w_query, w_key, w_value, w_out, gain, bias, src_key, src_tok, weight_num):
    n_x, n_kf = lax.axis_size("head"), lax.axis_size("kf")
    frames, tokens, width = key_states.shape
    full = gain.shape[0]
    vmem = pl.BlockSpec(memory_space=pltpu.VMEM)
    anywhere = pl.BlockSpec(memory_space=pltpu.HBM)
    bf16, f32 = jnp.bfloat16, jnp.float32
    dma = pltpu.SemaphoreType.DMA
    ko, ko_first = pl.pallas_call(
        functools.partial(attend, n_x),
        out_shape=(jax.ShapeDtypeStruct((2, width, PAD), bf16), jax.ShapeDtypeStruct((1, width, PAD), bf16)),
        in_specs=[anywhere] * 5 + [vmem, vmem],
        out_specs=(vmem, vmem),
        scratch_shapes=[
            pltpu.VMEM((frames, width, tokens), bf16),
            pltpu.VMEM((width, full), bf16), pltpu.VMEM((width, full), bf16), pltpu.VMEM((width, full), bf16),
            pltpu.VMEM((width, full), bf16),
            pltpu.VMEM((2, full, PAD), bf16),
            pltpu.VMEM((full, PAD), bf16),
            pltpu.VMEM((2, 6, 128, PAD), bf16),
            pltpu.VMEM((4, 2, 1280, 128), bf16),
            pltpu.VMEM((4, 2, width, PAD), bf16),
            pltpu.VMEM((3, 16, 6 * PAD), bf16),
            pltpu.VMEM((2, 5, 80, PAD), f32),
            pltpu.VMEM((2, 5, 1, PAD), f32),
            pltpu.VMEM((4, 2, width, PAD), bf16),
            pltpu.VMEM((4, width, width), bf16),
            pltpu.VMEM((4, width, width), bf16),
            pltpu.VMEM((2, full, 128), f32),
            dma((5,)), dma((2, 6)), dma((2, 6)), dma((3, 4, 2)), dma((3, 4, 2)),
            dma((6, 4)), dma((6, 4)), dma((3,)), dma((3,)),
        ],
        compiler_params=pltpu.CompilerParams(
            collective_id=0, has_side_effects=True, vmem_limit_bytes=56 * 2**20),
        name="attend",
    )(key_states.transpose(0, 2, 1), w_query.T, w_key.T, w_value.T, w_out,
      gain.reshape(full // 128, 128), bias.reshape(full // 128, 128))

    following = lax.ppermute(ko_first, "kf", [(i, i - 1) for i in range(1, n_kf)])

    def whole(shape):
        return pl.BlockSpec(shape, lambda j: (0,) * len(shape))

    n_out = weight_num.shape[0]
    each = n_out // frames
    keys_t, toks_t = src_key.transpose(0, 2, 1), src_tok.transpose(0, 2, 1)
    params = pltpu.CompilerParams(vmem_limit_bytes=40 * 2**20)
    cost = pl.CostEstimate(flops=2 * each * width * 2 * PAD * PAD, bytes_accessed=4_000_000, transcendentals=0)

    def part(base, shape):
        return pl.BlockSpec((each,) + shape, lambda j: (base, 0, 0))

    out = jax.ShapeDtypeStruct((n_out, width, tokens), bf16)
    made = [pltpu.VMEM((each, width, tokens), bf16), dma((each,))]
    key_out, half_done = pl.pallas_call(
        blend_first,
        grid=(1,),
        out_shape=(jax.ShapeDtypeStruct((frames, width, tokens), bf16), out),
        in_specs=[whole((2, width, PAD)), part(0, (2, tokens)), part(0, (2, tokens)), whole((n_out, tokens))],
        out_specs=(anywhere, anywhere),
        scratch_shapes=made + [pltpu.VMEM((frames, width, tokens), bf16), dma],
        compiler_params=params, cost_estimate=cost, name="blend_first",
    )(ko, keys_t, toks_t, weight_num)
    blended = pl.pallas_call(
        blend_second,
        grid=(1,),
        out_shape=out,
        in_specs=[whole((2, width, PAD)), whole((1, width, PAD)), part(1, (2, tokens)), part(1, (2, tokens)),
                  whole((n_out, tokens)), anywhere],
        out_specs=anywhere,
        scratch_shapes=made,
        input_output_aliases={5: 0},
        compiler_params=params, cost_estimate=cost, name="blend_second",
    )(ko, following, keys_t, toks_t, weight_num, half_done)
    return key_out.transpose(0, 2, 1), blended.transpose(0, 2, 1)


def solution(mesh):
    return jax.shard_map(
        body,
        mesh=mesh,
        in_specs=(
            P("kf", None, "head"),
            P(None, "head"),
            P(None, "head"),
            P(None, "head"),
            P("head", None),
            P(),
            P(),
            P("kf", None, None),
            P("kf", None, None),
            P("kf", None),
        ),
        out_specs=(P("kf", None, "head"), P("kf", None, "head")),
        check_vma=False,
    )
```
